32 devices in a mesh: aux: 4 (over z), ao: 8 (over y, x, core).
Axes of the slice: x: 2, y: 2, z: 4, core: 2. Of those that a mesh axis runs over, the one named last changes fastest.
Arguments:
- three_center: bfloat16 [512, 3, 3072], P('aux', None, 'ao'), may hold values from -6 to 6
- occ_green: bfloat16 [2, 3, 3], replicated, may hold values from -3.5 to 3.5
- virt_band: bfloat16 [2, 3072, 384], P(None, 'ao'), may hold values from -0.3125 to 0.3125
- tile_mask: int32 [4, 24], P('aux', 'ao'), may hold values 0 or 1
Outputs:
- polar: float32 [2, 512, 512], P(None, 'aux', 'ao')
The draws below stay inside these ranges and needn't reach their ends.
All inputs are finite; a program needn't handle non-finite values. No bound on the sum of `tile_mask` on one device may be relied on, other than what follows from the above.
Results may differ from the reference program's by a relative error of at most 0.0041.
Values may be sent and summed in bfloat16 or wider, within the bound.
No kernel may reach another device: no remote copies, remote signals or barrier semaphores. Data moves between devices by JAX's collectives and lax.ppermute only.
A program may use at most 64 MiB of HBM per device.

```python
import math
import jax
import jax.numpy as jnp
from jax import lax

TILE = 128
MU = 3
NTAU = 2
AUX = 512
AO = 3072


def set_ends(entries, rng, smallest, largest):
    place = [jax.random.randint(jax.random.fold_in(rng, axis), (), 0, length) for axis, length in enumerate(entries.shape)]
    widest = entries.shape.index(max(entries.shape))
    beside = place[:widest] + [(place[widest] + 1) % entries.shape[widest]] + place[widest + 1:]
    return entries.at[tuple(place)].set(smallest).at[tuple(beside)].set(largest)


def steps_of(rng, extent, shards, low, largest):
    gain = 1.0
    for position, parts in shards:
        draws = jax.random.uniform(jax.random.fold_in(jax.random.fold_in(rng, 6), position), (parts,), jnp.float32, low / len(shards), largest / len(shards))
        gain = gain * jnp.repeat(jnp.exp(draws), extent[position] // parts).reshape((-1,) + (1,) * (len(extent) - 1 - position))
    return gain


def noise(own_key, dims, width, limit, pieces=(), kind=jnp.bfloat16):
    drawn = jax.random.normal(own_key, dims, jnp.float32) * width
    if len(pieces) > 0:
        drawn = steps_of(own_key, dims, pieces, -0.22, 0.18) * drawn
    return jnp.clip(drawn, min=-limit, max=limit).astype(kind)


def setup_inputs(seed: int = 0) -> dict:
    arg_keys = jax.random.split(jax.random.key(seed), 5)
    return {
        "three_center": noise(arg_keys[0], (AUX, MU, AO), 1.0, 6.0, ((0, 4), (2, 8))),
        "occ_green": noise(arg_keys[1], (NTAU, MU, MU), MU ** -0.5, 3.5),
        "virt_band": noise(arg_keys[2], (NTAU, AO, 3 * TILE), (3 * TILE) ** -0.5, 0.3125, ((1, 8),)),
        "tile_mask": set_ends((jax.random.randint(arg_keys[3], (AUX // TILE, AO // TILE), 0, 4) < 3).astype(jnp.int32), jax.random.fold_in(arg_keys[3], 1), 0, 1),
    }


def reference(three_center, occ_green, virt_band, tile_mask):
    ptiles = AUX // TILE
    atiles = AO // TILE
    mask = tile_mask.astype(jnp.bfloat16)
    screened = (three_center.reshape(ptiles, TILE, MU, atiles, TILE) * mask[:, None, None, :, None]).reshape(AUX, MU, AO)
    flat = screened.reshape(AUX, MU * AO)
    band = virt_band.astype(jnp.float32).reshape(NTAU, atiles, TILE, 3 * TILE)
    green = occ_green.astype(jnp.float32)
    factor = 1.0 / math.sqrt(MU * AO)

    def one_block(block):
        rows = lax.dynamic_slice_in_dim(screened, (block * TILE).astype(jnp.int32), TILE, 0)
        product = jnp.einsum('tlm,pmn->tpln', green, rows.astype(jnp.float32)).astype(jnp.bfloat16)
        padded = jnp.pad(product, ((0, 0), (0, 0), (0, 0), (TILE, TILE))).reshape(NTAU, TILE, MU, atiles + 2, TILE)
        windows = jnp.concatenate([padded[:, :, :, :-2, :], padded[:, :, :, 1:-1, :], padded[:, :, :, 2:, :]], axis=4)
        dressed = jnp.einsum('tplsj,tsij->tplsi', windows.astype(jnp.float32), band).astype(jnp.bfloat16)
        dressed = dressed.reshape(NTAU * TILE, MU * AO)
        part = jnp.dot(dressed, flat.T, preferred_element_type=jnp.float32)
        return part.reshape(NTAU, TILE, AUX) * factor
    blocks = lax.map(one_block, jnp.arange(ptiles, dtype=jnp.int32))
    return jnp.transpose(blocks, (1, 0, 2, 3)).reshape(NTAU, AUX, AUX)
```

```python
import functools
import math

import jax
import jax.numpy as jnp
from jax import lax
from jax.experimental import pallas as pl
from jax.experimental.pallas import tpu as pltpu
from jax.sharding import PartitionSpec as P

VMEM = pl.BlockSpec(memory_space=pltpu.VMEM)
SMEM = pl.BlockSpec(memory_space=pltpu.SMEM)
NT = (((1,), (1,)), ((), ()))


def shape(dims, dtype):
    return jax.ShapeDtypeStruct(dims, dtype)


def screen_kernel(tile, mask_ref, raw_ref, out_ref, first_ref, last_ref):
    window, rows, cols = raw_ref.shape
    count = cols // tile
    for r in range(rows // tile):
        here = pl.ds(r * tile, tile)
        for l in range(window):
            for i in range(count):
                part = pl.ds(i * tile, tile)
                keep = mask_ref[r, i].astype(jnp.float32).astype(jnp.bfloat16)
                value = raw_ref[l, here, part] * keep
                out_ref[l, here, part] = value
                if i == 0:
                    first_ref[l, here, :] = value
                if i == count - 1:
                    last_ref[l, here, :] = value


def screen(mask, raw, tile):
    window, rows, cols = raw.shape
    edge = shape((window, rows, tile), raw.dtype)
    return pl.pallas_call(
        functools.partial(screen_kernel, tile),
        out_shape=[shape((window, rows, cols), raw.dtype), edge, edge],
        in_specs=[SMEM, VMEM],
        out_specs=[VMEM] * 3,
        name="screen",
    )(mask, raw)


def dress_kernel(tile, occ_ref, own_ref, before_ref, after_ref, band_ref, out_ref):
    window, rows, cols = own_ref.shape
    times = band_ref.shape[0]
    count = cols // tile
    tiles = []
    for i in range(count + 2):
        if i == 0:
            get = lambda m: before_ref[m]
        elif i == count + 1:
            get = lambda m: after_ref[m]
        else:
            get = lambda m, i=i: own_ref[m, :, pl.ds((i - 1) * tile, tile)]
        tiles.append([get(m).astype(jnp.float32) for m in range(window)])
    for t in range(times):
        products = []
        for l in range(window):
            row = []
            for group in tiles:
                total = occ_ref[t, l, 0] * group[0]
                for m in range(1, window):
                    total = total + occ_ref[t, l, m] * group[m]
                row.append(total.astype(jnp.bfloat16))
            products.append(jnp.concatenate(row, axis=1))
        tall = jnp.concatenate(products, axis=0)
        for i in range(count):
            part = pl.ds(i * tile, tile)
            value = lax.dot_general(
                tall[:, i * tile : (i + 3) * tile],
                band_ref[t, part, :],
                NT,
                preferred_element_type=jnp.float32,
            ).astype(jnp.bfloat16)
            for l in range(window):
                out_ref[l, pl.ds(t * rows, rows), part] = value[l * rows : (l + 1) * rows]


def dress(occ, own, before, after, band, tile):
    window, rows, cols = own.shape
    times = band.shape[0]
    return pl.pallas_call(
        functools.partial(dress_kernel, tile),
        out_shape=shape((window, times * rows, cols), jnp.bfloat16),
        in_specs=[SMEM] + [VMEM] * 4,
        out_specs=VMEM,
        name="dress",
    )(occ, own, before, after, band)


def share_kernel(offsets, width, dressed_ref, *refs):
    count = len(offsets)
    blocks, earlier = refs[:count], refs[count:-2]
    keep_ref, send_ref = refs[-2:]
    window, rows, _ = blocks[0].shape
    planes = lax.axis_size("aux")
    place = lax.axis_index("aux")
    core = lax.rem(lax.axis_index("ao"), 2)
    if earlier:
        keep_ref[...] = earlier[0][...]
        send_ref[...] = earlier[1][...]
    per = rows // (2 * width)
    for offset, block in zip(offsets, blocks):
        source = place + offset

        @pl.when((source >= 0) & (source < planes))
        def _(block=block, source=source):
            total = lax.dot_general(
                block[0], dressed_ref[0], NT, preferred_element_type=jnp.float32
            )
            for l in range(1, window):
                total += lax.dot_general(
                    block[l], dressed_ref[l], NT, preferred_element_type=jnp.float32
                )
            for j in range(per):
                low = total[2 * j * width : (2 * j + 1) * width]
                high = total[(2 * j + 1) * width : (2 * j + 2) * width]
                first = core == 0
                keep_ref[source * per + j] = jnp.where(first, low, high)
                send_ref[source * per + j] = jnp.where(first, high, low).astype(jnp.bfloat16)


def share(offsets, chips, width, dressed, blocks, earlier):
    dims = (chips, width, dressed.shape[1])
    args = [dressed, *blocks, *earlier]
    return pl.pallas_call(
        functools.partial(share_kernel, offsets, width),
        out_shape=[shape(dims, jnp.float32), shape(dims, jnp.bfloat16)],
        in_specs=[VMEM] * len(args),
        out_specs=[VMEM] * 2,
        name="share",
    )(*args)


def pair_kernel(keep_ref, got_ref, own_ref, *outs):
    chip = lax.axis_index("ao") // 2
    own_ref[...] = keep_ref[chip] + got_ref[chip].astype(jnp.float32)
    for k, out in enumerate(outs):
        other = chip ^ (k + 1)
        out[...] = (keep_ref[other] + got_ref[other].astype(jnp.float32)).astype(jnp.bfloat16)


def pair(keep, got):
    chips = keep.shape[0]
    dims = keep.shape[1:]
    return pl.pallas_call(
        pair_kernel,
        out_shape=[shape(dims, jnp.float32)] + [shape(dims, jnp.bfloat16)] * (chips - 1),
        in_specs=[VMEM] * 2,
        out_specs=[VMEM] * chips,
        name="pair",
    )(keep, got)


def finish_kernel(factor, own_ref, *refs):
    others, out_ref = refs[:-1], refs[-1]
    total = own_ref[...]
    for other in others:
        total += other[...].astype(jnp.float32)
    total *= factor
    rows = out_ref.shape[2]
    for t in range(out_ref.shape[0]):
        out_ref[t] = total[:, t * rows : (t + 1) * rows]


def finish(factor, times, own, others):
    width, both = own.shape
    return pl.pallas_call(
        functools.partial(finish_kernel, factor),
        out_shape=shape((times, width, both // times), jnp.float32),
        in_specs=[VMEM] * (1 + len(others)),
        out_specs=VMEM,
        name="finish",
    )(own, *others)


def shifted(x, axis, by):
    devices = lax.axis_size(axis)
    pairs = [(i, i + by) for i in range(devices) if 0 <= i + by < devices]
    return lax.ppermute(x, axis, pairs)


def body(three_center, occ_green, virt_band, tile_mask):
    rows, window, cols = three_center.shape
    times = virt_band.shape[0]
    tile = virt_band.shape[2] // 3
    planes, blocks = lax.axis_size("aux"), lax.axis_size("ao")
    chips = blocks // 2
    width = planes * rows // blocks
    factor = 1.0 / math.sqrt(window * cols * blocks)

    own, first, last = screen(tile_mask, three_center.transpose(1, 0, 2), tile)
    held = {0: own}
    for d in range(1, planes):
        hop, part = (d + 1) // 2, d // 2
        held[d] = shifted(held[part], "aux", -hop)
        held[-d] = shifted(held[-part], "aux", hop)
        if d == 1:
            before = shifted(last, "ao", 1)
            after = shifted(first, "ao", -1)
            dressed = dress(
                occ_green.astype(jnp.float32), own, before, after, virt_band, tile
            )
    near = [d for d in (0, 1, -1) if d in held]
    far = [d for d in held if d not in near]
    sums = share(near, chips, width, dressed, [held[d] for d in near], ())
    if far:
        sums = share(far, chips, width, dressed, [held[d] for d in far], sums)
    keep, send = sums
    got = lax.ppermute(send, "ao", [(i, i ^ 1) for i in range(blocks)])
    mine, *others = pair(keep, got)
    others = [
        lax.ppermute(other, "ao", [(i, i ^ (2 * k + 2)) for i in range(blocks)])
        for k, other in enumerate(others)
    ]
    return finish(factor, times, mine, others).transpose(0, 2, 1)


def solution(mesh):
    in_specs = (P("aux", None, "ao"), P(), P(None, "ao", None), P("aux", "ao"))
    out_specs = P(None, "aux", "ao")
    return jax.shard_map(body, mesh=mesh, in_specs=in_specs, out_specs=out_specs, check_vma=False)
```

```python
import functools
import math

import jax
import jax.numpy as jnp
from jax import lax
from jax.experimental import pallas as pl
from jax.experimental.pallas import tpu as pltpu
from jax.sharding import PartitionSpec as P

VMEM = pl.BlockSpec(memory_space=pltpu.VMEM)
SMEM = pl.BlockSpec(memory_space=pltpu.SMEM)
PARAMS = pltpu.CompilerParams(vmem_limit_bytes=16 * 1024 * 1024)
NT = (((1,), (1,)), ((), ()))


def shape(dims, dtype):
    return jax.ShapeDtypeStruct(dims, dtype)


def call(name, body, specs, outs, args):
    single = not isinstance(outs, (list, tuple))
    return pl.pallas_call(
        body,
        out_shape=outs,
        in_specs=specs,
        out_specs=VMEM if single else [VMEM] * len(outs),
        compiler_params=PARAMS,
        name=name,
    )(*args)


def is_even():
    return lax.rem(lax.axis_index("ao"), 2) == 0


def put_edges(even, first, last, inner_ref, outer_ref, here):
    inner_ref[here] = jnp.where(even, last, first)
    outer_ref[here] = jnp.where(even, first, last)


def screen_kernel(tile, mask_ref, raw_ref, out_ref, inner_ref, outer_ref):
    window, rows, cols = raw_ref.shape
    count = cols // tile
    even = is_even()
    for r in range(rows // tile):
        here = pl.ds(r * tile, tile)
        keep = [
            mask_ref[r, i].astype(jnp.float32).astype(jnp.bfloat16) for i in range(count)
        ]
        for l in range(window):
            values = []
            for i in range(count):
                part = pl.ds(i * tile, tile)
                values.append(raw_ref[l, here, part] * keep[i])
                out_ref[l, here, part] = values[i]
            put_edges(even, values[0], values[-1], inner_ref, outer_ref, (l, here))


def screen(mask, raw, tile):
    window, rows, cols = raw.shape
    edge = shape((window, rows, tile), raw.dtype)
    return call(
        "screen",
        functools.partial(screen_kernel, tile),
        [SMEM, VMEM],
        [shape(raw.shape, raw.dtype), edge, edge],
        (mask, raw),
    )


def edges_kernel(tile, full_ref, inner_ref, outer_ref):
    window, _, cols = full_ref.shape
    even = is_even()
    for l in range(window):
        first, last = full_ref[l, :, :tile], full_ref[l, :, cols - tile :]
        put_edges(even, first, last, inner_ref, outer_ref, (l,))


def edges(full, tile):
    window, rows, cols = full.shape
    edge = shape((window, rows, tile), full.dtype)
    return call("edges", functools.partial(edges_kernel, tile), [VMEM], [edge, edge], (full,))


def dress_kernel(tile, occ_ref, own_ref, inner_ref, outer_ref, band_ref, out_ref):
    window, rows, cols = own_ref.shape
    times = band_ref.shape[0]
    count = cols // tile
    place = lax.axis_index("ao")
    even = is_even()
    inside = ((place != 0) & (place != lax.axis_size("ao") - 1)).astype(jnp.float32)
    tiles = [[] for _ in range(count + 2)]
    for m in range(window):
        inner = inner_ref[m].astype(jnp.float32)
        outer = outer_ref[m].astype(jnp.float32) * inside
        tiles[0].append(jnp.where(even, outer, inner))
        tiles[-1].append(jnp.where(even, inner, outer))
        for i in range(count):
            tiles[i + 1].append(own_ref[m, :, pl.ds(i * tile, tile)].astype(jnp.float32))
    for t in range(times):
        products = []
        for l in range(window):
            row = []
            for group in tiles:
                total = occ_ref[t, l, 0] * group[0]
                for m in range(1, window):
                    total = total + occ_ref[t, l, m] * group[m]
                row.append(total.astype(jnp.bfloat16))
            products.append(jnp.concatenate(row, axis=1))
        tall = jnp.concatenate(products, axis=0)
        for i in range(count):
            value = lax.dot_general(
                tall[:, i * tile : (i + 3) * tile],
                band_ref[t, pl.ds(i * tile, tile), :],
                NT,
                preferred_element_type=jnp.float32,
            ).astype(jnp.bfloat16)
            for l in range(window):
                out_ref[pl.ds(t * rows, rows), pl.ds(l * cols + i * tile, tile)] = value[
                    l * rows : (l + 1) * rows
                ]


def dress(occ, own, inner, outer, band, tile):
    window, rows, cols = own.shape
    times = band.shape[0]
    return call(
        "dress",
        functools.partial(dress_kernel, tile),
        [SMEM] + [VMEM] * 4,
        shape((times * rows, window * cols), jnp.bfloat16),
        (occ, own, inner, outer, band),
    )


def share_kernel(sources, width, parts, *refs):
    count = len(sources)
    dressed, blocks = refs[:parts], refs[parts : parts + count]
    earlier = refs[parts + count : -2]
    keep_ref, send_ref = refs[-2:]
    window, rows, _ = blocks[0].shape
    planes = lax.axis_size("aux")
    place = lax.axis_index("aux")
    even = is_even()
    if earlier:
        keep_ref[...] = earlier[0][...]
        send_ref[...] = earlier[1][...]
    per = rows // (2 * width)
    for source_of, block in zip(sources, blocks):
        source = source_of(place)

        @pl.when((source >= 0) & (source < planes))
        def _(block=block, source=source):
            flat = jnp.concatenate([block[l] for l in range(window)], axis=1)
            at = 0
            for left in dressed:
                total = lax.dot_general(
                    flat, left[...], NT, preferred_element_type=jnp.float32
                )
                here = pl.ds(at, left.shape[0])
                at += left.shape[0]
                for j in range(per):
                    low = total[2 * j * width : (2 * j + 1) * width]
                    high = total[(2 * j + 1) * width : (2 * j + 2) * width]
                    row = source * per + j
                    keep_ref[row, :, here] = jnp.where(even, low, high)
                    send_ref[row, :, here] = jnp.where(even, high, low).astype(jnp.bfloat16)


def share(sources, chips, width, dressed, blocks, earlier):
    dims = (chips, width, sum(d.shape[0] for d in dressed))
    args = [*dressed, *blocks, *earlier]
    return call(
        "share",
        functools.partial(share_kernel, sources, width, len(dressed)),
        [VMEM] * len(args),
        [shape(dims, jnp.float32), shape(dims, jnp.bfloat16)],
        args,
    )


def pair_kernel(keep_ref, got_ref, own_ref, *outs):
    chip = lax.axis_index("ao") // 2
    own_ref[...] = keep_ref[chip] + got_ref[chip].astype(jnp.float32)
    for k, out in enumerate(outs):
        other = chip ^ (k + 1)
        out[...] = (keep_ref[other] + got_ref[other].astype(jnp.float32)).astype(jnp.bfloat16)


def pair(keep, got):
    chips = keep.shape[0]
    dims = keep.shape[1:]
    return call(
        "pair",
        pair_kernel,
        [VMEM] * 2,
        [shape(dims, jnp.float32)] + [shape(dims, jnp.bfloat16)] * (chips - 1),
        (keep, got),
    )


def total_kernel(factor, count, own_ref, *refs):
    others, outs = refs[:-count], refs[-count:]
    total = own_ref[...]
    for other in others:
        total += other[...].astype(jnp.float32)
    total *= factor
    times, _, rows = outs[0].shape
    for n, out in enumerate(outs):
        for t in range(times):
            at = (n * times + t) * rows
            out[t] = total[:, at : at + rows]


def total(factor, times, count, own, others):
    width, both = own.shape
    dims = (times, width, both // (times * count))
    return call(
        "total",
        functools.partial(total_kernel, factor, count),
        [VMEM] * (1 + len(others)),
        [shape(dims, jnp.float32)] * count,
        (own, *others),
    )


def choose_kernel(own_ref, got_ref, out_ref):
    place = lax.axis_index("aux")
    inner = (place == 1) | (place == 2)
    out_ref[...] = jnp.where(inner, own_ref[...], got_ref[...])


def choose(own, got):
    return call("choose", choose_kernel, [VMEM] * 2, shape(own.shape, own.dtype), (own, got))


def shifted(x, axis, by):
    devices = lax.axis_size(axis)
    pairs = [(i, i + by) for i in range(devices) if 0 <= i + by < devices]
    return lax.ppermute(x, axis, pairs)


def body(three_center, occ_green, virt_band, tile_mask):
    rows, window, cols = three_center.shape
    times = virt_band.shape[0]
    tile = virt_band.shape[2] // 3
    planes, blocks = lax.axis_size("aux"), lax.axis_size("ao")
    chips = blocks // 2
    width = planes * rows // blocks
    factor = 1.0 / math.sqrt(window * cols * blocks)
    mates = [(i, i ^ 1) for i in range(blocks)]
    nexts = [(i, (i + 1 if i % 2 else i - 1) % blocks) for i in range(blocks)]

    def halo(inner, outer):
        return lax.ppermute(inner, "ao", mates), lax.ppermute(outer, "ao", nexts)

    occ = occ_green.astype(jnp.float32)
    own, inner, outer = screen(tile_mask, three_center.transpose(1, 0, 2), tile)
    if planes == 4:
        swap = [(0, 1), (1, 0), (2, 3), (3, 2)]
        beside = lax.ppermute(own, "aux", swap)
        second = lax.ppermute(own, "aux", [(0, 2), (3, 1), (1, 0), (2, 3)])
        across = lax.ppermute(own, "aux", [(1, 2), (2, 1), (0, 0), (3, 3)])
        dressed = [
            dress(occ, own, *halo(inner, outer), virt_band, tile),
            dress(occ, beside, *halo(*edges(beside, tile)), virt_band, tile),
        ]
        near = {0: (lambda z: z, own), 1: (lambda z: z ^ 1, beside)}
        far = {2: (lambda z: 3 - z, across), 3: (lambda z: z ^ 2, second)}
    else:
        held = {0: own}
        for d in range(1, planes):
            hop, part = (d + 1) // 2, d // 2
            held[d] = shifted(held[part], "aux", -hop)
            held[-d] = shifted(held[-part], "aux", hop)
        dressed = [dress(occ, own, *halo(inner, outer), virt_band, tile)]
        plan = {d: (lambda z, d=d: z + d, block) for d, block in held.items()}
        near = {d: plan[d] for d in plan if abs(d) < 2}
        far = {d: plan[d] for d in plan if abs(d) >= 2}
    sums = ()
    for group in (near, far):
        if group:
            sources, held = zip(*group.values())
            sums = share(sources, chips, width, dressed, held, sums)
    keep, send = sums
    mine, *others = pair(keep, lax.ppermute(send, "ao", mates))
    others = [
        lax.ppermute(other, "ao", [(i, i ^ (2 * k + 2)) for i in range(blocks)])
        for k, other in enumerate(others)
    ]
    outs = total(factor, times, len(dressed), mine, others)
    if planes == 4:
        out = choose(outs[0], lax.ppermute(outs[1], "aux", swap))
    else:
        out = outs[0]
    return out.transpose(0, 2, 1)


def solution(mesh):
    in_specs = (P("aux", None, "ao"), P(), P(None, "ao", None), P("aux", "ao"))
    out_specs = P(None, "aux", "ao")
    return jax.shard_map(body, mesh=mesh, in_specs=in_specs, out_specs=out_specs, check_vma=False)
```

```python
import functools
import math

import jax
import jax.numpy as jnp
from jax import lax
from jax.experimental import pallas as pl
from jax.experimental.pallas import tpu as pltpu
from jax.sharding import PartitionSpec as P

VMEM = pl.BlockSpec(memory_space=pltpu.VMEM)
PARAMS = pltpu.CompilerParams(vmem_limit_bytes=16 * 1024 * 1024)
NT = (((1,), (1,)), ((), ()))


def shape(dims, dtype):
    return jax.ShapeDtypeStruct(dims, dtype)


def call(name, body, specs, outs, args):
    single = not isinstance(outs, (list, tuple))
    return pl.pallas_call(
        body,
        out_shape=outs,
        in_specs=specs,
        out_specs=VMEM if single else [VMEM] * len(outs),
        compiler_params=PARAMS,
        name=name,
    )(*args)


def is_even():
    return lax.rem(lax.axis_index("ao"), 2) == 0


def edge_kernel(tile, inner, full_ref, *refs):
    out_ref = refs[-1]
    window, _, cols = full_ref.shape
    at_end = is_even() if inner else jnp.logical_not(is_even())
    for l in range(window):
        first, last = full_ref[l, :, :tile], full_ref[l, :, cols - tile :]
        out_ref[l] = jnp.where(at_end, last, first)


def edge(inner, full, tile, after=()):
    window, rows, cols = full.shape
    return pl.pallas_call(
        functools.partial(edge_kernel, tile, inner),
        out_shape=shape((window, rows, tile), full.dtype),
        in_specs=[VMEM] + [pl.BlockSpec(memory_space=pl.ANY)] * len(after),
        out_specs=VMEM,
        compiler_params=PARAMS,
        name="edge",
    )(full, *after)


def dress_kernel(tile, occ_ref, own_ref, inner_ref, outer_ref, band_ref, *refs):
    out_ref = refs[-1]
    window, rows, cols = own_ref.shape
    times = band_ref.shape[0]
    count = cols // tile
    place = lax.axis_index("ao")
    even = is_even()
    inside = ((place != 0) & (place != lax.axis_size("ao") - 1)).astype(jnp.float32)
    tiles = [[] for _ in range(count + 2)]
    for m in range(window):
        inner = inner_ref[m].astype(jnp.float32)
        outer = outer_ref[m].astype(jnp.float32) * inside
        tiles[0].append(jnp.where(even, outer, inner))
        tiles[-1].append(jnp.where(even, inner, outer))
        for i in range(count):
            tiles[i + 1].append(own_ref[m, :, pl.ds(i * tile, tile)].astype(jnp.float32))
    green = [occ_ref[l].astype(jnp.float32) for l in range(window)]
    for t in range(times):
        products = []
        for l in range(window):
            row = []
            gains = [
                jnp.broadcast_to(green[l][t : t + 1, m : m + 1], (rows, tile))
                for m in range(window)
            ]
            for group in tiles:
                total = gains[0] * group[0]
                for m in range(1, window):
                    total = total + gains[m] * group[m]
                row.append(total.astype(jnp.bfloat16))
            products.append(jnp.concatenate(row, axis=1))
        tall = jnp.concatenate(products, axis=0)
        for i in range(count):
            value = lax.dot_general(
                tall[:, i * tile : (i + 3) * tile],
                band_ref[t, pl.ds(i * tile, tile), :],
                NT,
                preferred_element_type=jnp.float32,
            ).astype(jnp.bfloat16)
            for l in range(window):
                out_ref[pl.ds(t * rows, rows), pl.ds(l * cols + i * tile, tile)] = value[
                    l * rows : (l + 1) * rows
                ]


def dress(occ, own, inner, outer, band, tile, after=()):
    window, rows, cols = own.shape
    times = band.shape[0]
    return call(
        "dress",
        functools.partial(dress_kernel, tile),
        [VMEM] * 5 + [pl.BlockSpec(memory_space=pl.ANY)] * len(after),
        shape((times * rows, window * cols), jnp.bfloat16),
        (occ, own, inner, outer, band, *after),
    )


def share_kernel(sources, width, parts, *refs):
    count = len(sources)
    dressed, blocks = refs[:parts], refs[parts : parts + count]
    earlier = refs[parts + count : -2]
    keep_ref, send_ref = refs[-2:]
    window, rows, _ = blocks[0].shape
    planes = lax.axis_size("aux")
    place = lax.axis_index("aux")
    even = is_even()
    if earlier:
        keep_ref[...] = earlier[0][...]
        send_ref[...] = earlier[1][...]
    per = rows // (2 * width)

    def flat(block):
        return jnp.concatenate([block[l] for l in range(window)], axis=1)

    def put(total, source, here):
        for j in range(per):
            low = total[2 * j * width : (2 * j + 1) * width]
            high = total[(2 * j + 1) * width : (2 * j + 2) * width]
            row = source * per + j
            keep_ref[row, :, here] = jnp.where(even, low, high)
            send_ref[row, :, here] = jnp.where(even, high, low).astype(jnp.bfloat16)

    at = 0
    for left in dressed:
        here = pl.ds(at, left.shape[0])
        at += left.shape[0]
        if parts > 1:
            tall = jnp.concatenate([flat(block) for block in blocks], axis=0)
            total = lax.dot_general(tall, left[...], NT, preferred_element_type=jnp.float32)
            for n, source_of in enumerate(sources):
                put(total[n * rows : (n + 1) * rows], source_of(place), here)
            continue
        for source_of, block in zip(sources, blocks):
            source = source_of(place)

            @pl.when((source >= 0) & (source < planes))
            def _(block=block, source=source, left=left, here=here):
                put(
                    lax.dot_general(
                        flat(block), left[...], NT, preferred_element_type=jnp.float32
                    ),
                    source,
                    here,
                )


def share(sources, chips, width, dressed, blocks, earlier):
    dims = (chips, width, sum(d.shape[0] for d in dressed))
    args = [*dressed, *blocks, *earlier]
    return call(
        "share",
        functools.partial(share_kernel, sources, width, len(dressed)),
        [VMEM] * len(args),
        [shape(dims, jnp.float32), shape(dims, jnp.bfloat16)],
        args,
    )


def pair_kernel(keep_ref, got_ref, own_ref, *outs):
    chip = lax.axis_index("ao") // 2
    own_ref[...] = keep_ref[chip] + got_ref[chip].astype(jnp.float32)
    for k, out in enumerate(outs):
        other = chip ^ (k + 1)
        out[...] = (keep_ref[other] + got_ref[other].astype(jnp.float32)).astype(jnp.bfloat16)


def pair(keep, got):
    chips = keep.shape[0]
    dims = keep.shape[1:]
    return call(
        "pair",
        pair_kernel,
        [VMEM] * 2,
        [shape(dims, jnp.float32)] + [shape(dims, jnp.bfloat16)] * (chips - 1),
        (keep, got),
    )


def total_kernel(factor, count, own_ref, *refs):
    others, outs = refs[:-count], refs[-count:]
    total = own_ref[...]
    for other in others:
        total += other[...].astype(jnp.float32)
    total *= factor
    times, _, rows = outs[0].shape
    for n, out in enumerate(outs):
        for t in range(times):
            at = (n * times + t) * rows
            out[t] = total[:, at : at + rows]


def total(factor, times, count, own, others):
    width, both = own.shape
    dims = (times, width, both // (times * count))
    return call(
        "total",
        functools.partial(total_kernel, factor, count),
        [VMEM] * (1 + len(others)),
        [shape(dims, jnp.float32)] * count,
        (own, *others),
    )


def choose_kernel(own_ref, got_ref, out_ref):
    place = lax.axis_index("aux")
    inner = (place == 1) | (place == 2)
    out_ref[...] = jnp.where(inner, own_ref[...], got_ref[...])


def choose(own, got):
    return call("choose", choose_kernel, [VMEM] * 2, shape(own.shape, own.dtype), (own, got))


def shifted(x, axis, by):
    devices = lax.axis_size(axis)
    pairs = [(i, i + by) for i in range(devices) if 0 <= i + by < devices]
    return lax.ppermute(x, axis, pairs)


def body(three_center, occ_green, virt_band, tile_mask):
    rows, window, cols = three_center.shape
    times = virt_band.shape[0]
    tile = virt_band.shape[2] // 3
    planes, blocks = lax.axis_size("aux"), lax.axis_size("ao")
    chips = blocks // 2
    width = planes * rows // blocks
    factor = 1.0 / math.sqrt(window * cols * blocks)
    mates = [(i, i ^ 1) for i in range(blocks)]
    nexts = [(i, (i + 1 if i % 2 else i - 1) % blocks) for i in range(blocks)]

    def halo(full):
        inner, outer = edge(True, full, tile), edge(False, full, tile)
        return lax.ppermute(inner, "ao", mates), lax.ppermute(outer, "ao", nexts)

    occ = occ_green.transpose(1, 0, 2)
    mask = tile_mask.astype(jnp.bfloat16)[None, :, None, :, None]
    split = (window, rows // tile, tile, cols // tile, tile)
    own = three_center.transpose(1, 0, 2).reshape(split) * mask
    own = own.reshape(window, rows, cols)
    if planes == 4:
        swap = [(0, 1), (1, 0), (2, 3), (3, 2)]
        across = lax.ppermute(own, "aux", [(1, 2), (2, 1), (0, 0), (3, 3)])
        beside = lax.ppermute(own, "aux", swap)
        second = lax.ppermute(own, "aux", [(0, 2), (3, 1), (1, 0), (2, 3)])
        facing = edge(False, beside, tile)
        dressed = [dress(occ, own, *halo(own), virt_band, tile, (facing,))]
        outer = lax.ppermute(facing, "ao", nexts)
        inner = lax.ppermute(edge(True, beside, tile, dressed), "ao", mates)
        dressed.append(dress(occ, beside, inner, outer, virt_band, tile))
        near = {0: (lambda z: z, own), 1: (lambda z: z ^ 1, beside)}
        far = {2: (lambda z: 3 - z, across), 3: (lambda z: z ^ 2, second)}
    else:
        held = {0: own}
        for d in range(1, planes):
            hop, part = (d + 1) // 2, d // 2
            held[d] = shifted(held[part], "aux", -hop)
            held[-d] = shifted(held[-part], "aux", hop)
        dressed = [dress(occ, own, *halo(own), virt_band, tile)]
        plan = {d: (lambda z, d=d: z + d, block) for d, block in held.items()}
        near = {d: plan[d] for d in plan if abs(d) < 2}
        far = {d: plan[d] for d in plan if abs(d) >= 2}
    sums = ()
    for group in (near, far):
        if group:
            sources, held = zip(*group.values())
            sums = share(sources, chips, width, dressed, held, sums)
    keep, send = sums
    mine, *others = pair(keep, lax.ppermute(send, "ao", mates))
    others = [
        lax.ppermute(other, "ao", [(i, i ^ (2 * k + 2)) for i in range(blocks)])
        for k, other in enumerate(others)
    ]
    outs = total(factor, times, len(dressed), mine, others)
    if planes == 4:
        out = choose(outs[0], lax.ppermute(outs[1], "aux", swap))
    else:
        out = outs[0]
    return out.transpose(0, 2, 1)


def solution(mesh):
    in_specs = (P("aux", None, "ao"), P(), P(None, "ao", None), P("aux", "ao"))
    out_specs = P(None, "aux", "ao")
    return jax.shard_map(body, mesh=mesh, in_specs=in_specs, out_specs=out_specs, check_vma=False)
```

```python
import functools
import math

import jax
import jax.numpy as jnp
from jax import lax
from jax.experimental import pallas as pl
from jax.experimental.pallas import tpu as pltpu
from jax.sharding import PartitionSpec as P

VMEM = pl.BlockSpec(memory_space=pltpu.VMEM)
PARAMS = pltpu.CompilerParams(vmem_limit_bytes=16 * 1024 * 1024)
NT = (((1,), (1,)), ((), ()))


def shape(dims, dtype):
    return jax.ShapeDtypeStruct(dims, dtype)


def call(name, body, specs, outs, args):
    single = not isinstance(outs, (list, tuple))
    return pl.pallas_call(
        body,
        out_shape=outs,
        in_specs=specs,
        out_specs=VMEM if single else [VMEM] * len(outs),
        compiler_params=PARAMS,
        name=name,
    )(*args)


def is_even():
    return lax.rem(lax.axis_index("ao"), 2) == 0


def edge_kernel(tile, inner, full_ref, *refs):
    out_ref = refs[-1]
    window, _, cols = full_ref.shape
    at_end = is_even() if inner else jnp.logical_not(is_even())
    for l in range(window):
        first, last = full_ref[l, :, :tile], full_ref[l, :, cols - tile :]
        out_ref[l] = jnp.where(at_end, last, first)


def edge(inner, full, tile, after=()):
    window, rows, cols = full.shape
    return pl.pallas_call(
        functools.partial(edge_kernel, tile, inner),
        out_shape=shape((window, rows, tile), full.dtype),
        in_specs=[VMEM] + [pl.BlockSpec(memory_space=pl.ANY)] * len(after),
        out_specs=VMEM,
        compiler_params=PARAMS,
        name="edge",
    )(full, *after)


def dress_kernel(tile, occ_ref, own_ref, inner_ref, outer_ref, band_ref, *refs):
    out_ref = refs[-1]
    window, rows, cols = own_ref.shape
    times = band_ref.shape[0]
    count = cols // tile
    place = lax.axis_index("ao")
    even = is_even()
    inside = ((place != 0) & (place != lax.axis_size("ao") - 1)).astype(jnp.float32)
    tiles = [[] for _ in range(count + 2)]
    for m in range(window):
        inner = inner_ref[m].astype(jnp.float32)
        outer = outer_ref[m].astype(jnp.float32) * inside
        tiles[0].append(jnp.where(even, outer, inner))
        tiles[-1].append(jnp.where(even, inner, outer))
        for i in range(count):
            tiles[i + 1].append(own_ref[m, :, pl.ds(i * tile, tile)].astype(jnp.float32))
    green = [occ_ref[l].astype(jnp.float32) for l in range(window)]
    for t in range(times):
        products = []
        for l in range(window):
            row = []
            gains = [
                jnp.broadcast_to(green[l][t : t + 1, m : m + 1], (rows, tile))
                for m in range(window)
            ]
            for group in tiles:
                total = gains[0] * group[0]
                for m in range(1, window):
                    total = total + gains[m] * group[m]
                row.append(total.astype(jnp.bfloat16))
            products.append(jnp.concatenate(row, axis=1))
        tall = jnp.concatenate(products, axis=0)
        for i in range(count):
            value = lax.dot_general(
                tall[:, i * tile : (i + 3) * tile],
                band_ref[t, pl.ds(i * tile, tile), :],
                NT,
                preferred_element_type=jnp.float32,
            ).astype(jnp.bfloat16)
            for l in range(window):
                out_ref[pl.ds(t * rows, rows), pl.ds(l * cols + i * tile, tile)] = value[
                    l * rows : (l + 1) * rows
                ]


def dress(occ, own, inner, outer, band, tile, after=()):
    window, rows, cols = own.shape
    times = band.shape[0]
    return call(
        "dress",
        functools.partial(dress_kernel, tile),
        [VMEM] * 5 + [pl.BlockSpec(memory_space=pl.ANY)] * len(after),
        shape((times * rows, window * cols), jnp.bfloat16),
        (occ, own, inner, outer, band, *after),
    )


def share_kernel(sources, width, parts, *refs):
    count = len(sources)
    dressed, blocks = refs[:parts], refs[parts : parts + count]
    earlier = refs[parts + count : -2]
    keep_ref, send_ref = refs[-2:]
    window, rows, _ = blocks[0].shape
    planes = lax.axis_size("aux")
    place = lax.axis_index("aux")
    even = is_even()
    if earlier:
        keep_ref[...] = earlier[0][...]
        send_ref[...] = earlier[1][...]
    per = rows // (2 * width)

    def flat(block):
        return jnp.concatenate([block[l] for l in range(window)], axis=1)

    def put(total, source, here):
        for j in range(per):
            low = total[2 * j * width : (2 * j + 1) * width]
            high = total[(2 * j + 1) * width : (2 * j + 2) * width]
            row = source * per + j
            keep_ref[row, :, here] = jnp.where(even, low, high)
            send_ref[row, :, here] = jnp.where(even, high, low).astype(jnp.bfloat16)

    at = 0
    for left in dressed:
        here = pl.ds(at, left.shape[0])
        at += left.shape[0]
        if parts > 1:
            tall = jnp.concatenate([flat(block) for block in blocks], axis=0)
            total = lax.dot_general(tall, left[...], NT, preferred_element_type=jnp.float32)
            for n, source_of in enumerate(sources):
                put(total[n * rows : (n + 1) * rows], source_of(place), here)
            continue
        for source_of, block in zip(sources, blocks):
            source = source_of(place)

            @pl.when((source >= 0) & (source < planes))
            def _(block=block, source=source, left=left, here=here):
                put(
                    lax.dot_general(
                        flat(block), left[...], NT, preferred_element_type=jnp.float32
                    ),
                    source,
                    here,
                )


def share(sources, chips, width, dressed, blocks, earlier):
    dims = (chips, width, sum(d.shape[0] for d in dressed))
    args = [*dressed, *blocks, *earlier]
    return call(
        "share",
        functools.partial(share_kernel, sources, width, len(dressed)),
        [VMEM] * len(args),
        [shape(dims, jnp.float32), shape(dims, jnp.bfloat16)],
        args,
    )


def pair_kernel(keep_ref, got_ref, own_ref, *outs):
    chip = lax.axis_index("ao") // 2
    own_ref[...] = keep_ref[chip] + got_ref[chip].astype(jnp.float32)
    for k, out in enumerate(outs):
        other = chip ^ (k + 1)
        out[...] = (keep_ref[other] + got_ref[other].astype(jnp.float32)).astype(jnp.bfloat16)


def pair(keep, got):
    chips = keep.shape[0]
    dims = keep.shape[1:]
    return call(
        "pair",
        pair_kernel,
        [VMEM] * 2,
        [shape(dims, jnp.float32)] + [shape(dims, jnp.bfloat16)] * (chips - 1),
        (keep, got),
    )


def total_kernel(factor, count, own_ref, *refs):
    others, outs = refs[:-count], refs[-count:]
    total = own_ref[...]
    for other in others:
        total += other[...].astype(jnp.float32)
    total *= factor
    times, _, rows = outs[0].shape
    for n, out in enumerate(outs):
        for t in range(times):
            at = (n * times + t) * rows
            out[t] = total[:, at : at + rows].astype(out.dtype)


def total(factor, times, count, own, others):
    width, both = own.shape
    dims = (times, width, both // (times * count))
    return call(
        "total",
        functools.partial(total_kernel, factor, count),
        [VMEM] * (1 + len(others)),
        [shape(dims, jnp.float32)] + [shape(dims, jnp.bfloat16)] * (count - 1),
        (own, *others),
    )


def choose_kernel(own_ref, got_ref, out_ref):
    place = lax.axis_index("aux")
    inner = (place == 1) | (place == 2)
    out_ref[...] = jnp.where(inner, own_ref[...], got_ref[...].astype(jnp.float32))


def choose(own, got):
    return call("choose", choose_kernel, [VMEM] * 2, shape(own.shape, own.dtype), (own, got))


def shifted(x, axis, by):
    devices = lax.axis_size(axis)
    pairs = [(i, i + by) for i in range(devices) if 0 <= i + by < devices]
    return lax.ppermute(x, axis, pairs)


def body(three_center, occ_green, virt_band, tile_mask):
    rows, window, cols = three_center.shape
    times = virt_band.shape[0]
    tile = virt_band.shape[2] // 3
    planes, blocks = lax.axis_size("aux"), lax.axis_size("ao")
    chips = blocks // 2
    width = planes * rows // blocks
    factor = 1.0 / math.sqrt(window * cols * blocks)
    mates = [(i, i ^ 1) for i in range(blocks)]
    nexts = [(i, (i + 1 if i % 2 else i - 1) % blocks) for i in range(blocks)]

    def halo(full):
        inner, outer = edge(True, full, tile), edge(False, full, tile)
        return lax.ppermute(inner, "ao", mates), lax.ppermute(outer, "ao", nexts)

    occ = occ_green.transpose(1, 0, 2)
    mask = tile_mask.astype(jnp.bfloat16)[None, :, None, :, None]
    split = (window, rows // tile, tile, cols // tile, tile)
    own = three_center.transpose(1, 0, 2).reshape(split) * mask
    own = own.reshape(window, rows, cols)
    if planes == 4:
        swap = [(0, 1), (1, 0), (2, 3), (3, 2)]
        across = lax.ppermute(own, "aux", [(1, 2), (2, 1), (0, 0), (3, 3)])
        beside = lax.ppermute(own, "aux", swap)
        second = lax.ppermute(own, "aux", [(0, 2), (3, 1), (1, 0), (2, 3)])
        facing = edge(False, beside, tile)
        dressed = [dress(occ, own, *halo(own), virt_band, tile, (facing,))]
        outer = lax.ppermute(facing, "ao", nexts)
        inner = lax.ppermute(edge(True, beside, tile, dressed), "ao", mates)
        dressed.append(dress(occ, beside, inner, outer, virt_band, tile))
        near = {0: (lambda z: z, own), 1: (lambda z: z ^ 1, beside)}
        far = {3: (lambda z: z ^ 2, second), 2: (lambda z: 3 - z, across)}
    else:
        held = {0: own}
        for d in range(1, planes):
            hop, part = (d + 1) // 2, d // 2
            held[d] = shifted(held[part], "aux", -hop)
            held[-d] = shifted(held[-part], "aux", hop)
        dressed = [dress(occ, own, *halo(own), virt_band, tile)]
        plan = {d: (lambda z, d=d: z + d, block) for d, block in held.items()}
        near = {d: plan[d] for d in plan if abs(d) < 2}
        far = {d: plan[d] for d in plan if abs(d) >= 2}
    sums = ()
    for group in (near, far):
        if group:
            sources, held = zip(*group.values())
            sums = share(sources, chips, width, dressed, held, sums)
    keep, send = sums
    mine, *others = pair(keep, lax.ppermute(send, "ao", mates))
    others = [
        lax.ppermute(other, "ao", [(i, i ^ (2 * k + 2)) for i in range(blocks)])
        for k, other in enumerate(others)
    ]
    outs = total(factor, times, len(dressed), mine, others)
    if planes == 4:
        out = choose(outs[0], lax.ppermute(outs[1], "aux", swap))
    else:
        out = outs[0]
    return out.transpose(0, 2, 1)


def solution(mesh):
    in_specs = (P("aux", None, "ao"), P(), P(None, "ao", None), P("aux", "ao"))
    out_specs = P(None, "aux", "ao")
    return jax.shard_map(body, mesh=mesh, in_specs=in_specs, out_specs=out_specs, check_vma=False)
```

```python
import functools
import math

import jax
import jax.numpy as jnp
from jax import lax
from jax.experimental import pallas as pl
from jax.experimental.pallas import tpu as pltpu
from jax.sharding import PartitionSpec as P

VMEM = pl.BlockSpec(memory_space=pltpu.VMEM)
PARAMS = pltpu.CompilerParams(vmem_limit_bytes=16 * 1024 * 1024)
NT = (((1,), (1,)), ((), ()))


def shape(dims, dtype):
    return jax.ShapeDtypeStruct(dims, dtype)


def call(name, body, specs, outs, args):
    single = not isinstance(outs, (list, tuple))
    return pl.pallas_call(
        body,
        out_shape=outs,
        in_specs=specs,
        out_specs=VMEM if single else [VMEM] * len(outs),
        compiler_params=PARAMS,
        name=name,
    )(*args)


def is_even():
    return lax.rem(lax.axis_index("ao"), 2) == 0


def edge_kernel(tile, inner, full_ref, *refs):
    out_ref = refs[-1]
    window, _, cols = full_ref.shape
    at_end = is_even() if inner else jnp.logical_not(is_even())
    for l in range(window):
        first, last = full_ref[l, :, :tile], full_ref[l, :, cols - tile :]
        out_ref[l] = jnp.where(at_end, last, first)


def edge(inner, full, tile, after=()):
    window, rows, cols = full.shape
    return pl.pallas_call(
        functools.partial(edge_kernel, tile, inner),
        out_shape=shape((window, rows, tile), full.dtype),
        in_specs=[VMEM] + [pl.BlockSpec(memory_space=pl.ANY)] * len(after),
        out_specs=VMEM,
        compiler_params=PARAMS,
        name="edge",
    )(full, *after)


def dress_kernel(tile, occ_ref, own_ref, inner_ref, outer_ref, band_ref, *refs):
    out_ref = refs[-1]
    window, rows, cols = own_ref.shape
    times = band_ref.shape[0]
    count = cols // tile
    place = lax.axis_index("ao")
    even = is_even()
    inside = ((place != 0) & (place != lax.axis_size("ao") - 1)).astype(jnp.float32)
    tiles = [[] for _ in range(count + 2)]
    for m in range(window):
        inner = inner_ref[m].astype(jnp.float32)
        outer = outer_ref[m].astype(jnp.float32) * inside
        tiles[0].append(jnp.where(even, outer, inner))
        tiles[-1].append(jnp.where(even, inner, outer))
        for i in range(count):
            tiles[i + 1].append(own_ref[m, :, pl.ds(i * tile, tile)].astype(jnp.float32))
    green = [occ_ref[l].astype(jnp.float32) for l in range(window)]
    for t in range(times):
        products = []
        for l in range(window):
            row = []
            gains = [
                jnp.broadcast_to(green[l][t : t + 1, m : m + 1], (rows, tile))
                for m in range(window)
            ]
            for group in tiles:
                total = gains[0] * group[0]
                for m in range(1, window):
                    total = total + gains[m] * group[m]
                row.append(total.astype(jnp.bfloat16))
            products.append(jnp.concatenate(row, axis=1))
        tall = jnp.concatenate(products, axis=0)
        for i in range(count):
            value = lax.dot_general(
                tall[:, i * tile : (i + 3) * tile],
                band_ref[t, pl.ds(i * tile, tile), :],
                NT,
                preferred_element_type=jnp.float32,
            ).astype(jnp.bfloat16)
            for l in range(window):
                out_ref[pl.ds(t * rows, rows), pl.ds(l * cols + i * tile, tile)] = value[
                    l * rows : (l + 1) * rows
                ]


def dress(occ, own, inner, outer, band, tile, after=()):
    window, rows, cols = own.shape
    times = band.shape[0]
    return call(
        "dress",
        functools.partial(dress_kernel, tile),
        [VMEM] * 5 + [pl.BlockSpec(memory_space=pl.ANY)] * len(after),
        shape((times * rows, window * cols), jnp.bfloat16),
        (occ, own, inner, outer, band, *after),
    )


def share_kernel(sources, width, parts, *refs):
    count = len(sources)
    dressed, blocks = refs[:parts], refs[parts : parts + count]
    earlier = refs[parts + count : -2]
    keep_ref, send_ref = refs[-2:]
    window, rows, _ = blocks[0].shape
    planes = lax.axis_size("aux")
    place = lax.axis_index("aux")
    even = is_even()
    if earlier:
        keep_ref[...] = earlier[0][...]
        send_ref[...] = earlier[1][...]
    per = rows // (2 * width)

    def flat(block):
        return jnp.concatenate([block[l] for l in range(window)], axis=1)

    def put(total, source, here):
        for j in range(per):
            low = total[2 * j * width : (2 * j + 1) * width]
            high = total[(2 * j + 1) * width : (2 * j + 2) * width]
            row = source * per + j
            keep_ref[row, :, here] = jnp.where(even, low, high)
            send_ref[row, :, here] = jnp.where(even, high, low).astype(jnp.bfloat16)

    at = 0
    for left in dressed:
        here = pl.ds(at, left.shape[0])
        at += left.shape[0]
        if parts > 1:
            tall = jnp.concatenate([flat(block) for block in blocks], axis=0)
            total = lax.dot_general(tall, left[...], NT, preferred_element_type=jnp.float32)
            for n, source_of in enumerate(sources):
                put(total[n * rows : (n + 1) * rows], source_of(place), here)
            continue
        for source_of, block in zip(sources, blocks):
            source = source_of(place)

            @pl.when((source >= 0) & (source < planes))
            def _(block=block, source=source, left=left, here=here):
                put(
                    lax.dot_general(
                        flat(block), left[...], NT, preferred_element_type=jnp.float32
                    ),
                    source,
                    here,
                )


def share(sources, chips, width, dressed, blocks, earlier):
    dims = (chips, width, sum(d.shape[0] for d in dressed))
    args = [*dressed, *blocks, *earlier]
    return call(
        "share",
        functools.partial(share_kernel, sources, width, len(dressed)),
        [VMEM] * len(args),
        [shape(dims, jnp.float32), shape(dims, jnp.bfloat16)],
        args,
    )


def farthest_first(chips):
    return range(chips - 1, 0, -1)


def pair_kernel(keep_ref, got_ref, own_ref, *outs):
    chip = lax.axis_index("ao") // 2
    own_ref[...] = keep_ref[chip] + got_ref[chip].astype(jnp.float32)
    for k, out in zip(farthest_first(keep_ref.shape[0]), outs):
        other = chip ^ k
        out[...] = (keep_ref[other] + got_ref[other].astype(jnp.float32)).astype(jnp.bfloat16)


def pair(keep, got):
    chips = keep.shape[0]
    dims = keep.shape[1:]
    return call(
        "pair",
        pair_kernel,
        [VMEM] * 2,
        [shape(dims, jnp.float32)] + [shape(dims, jnp.bfloat16)] * (chips - 1),
        (keep, got),
    )


def total_kernel(factor, count, own_ref, *refs):
    others, outs = refs[:-count], refs[-count:]
    total = own_ref[...]
    for other in others:
        total += other[...].astype(jnp.float32)
    total *= factor
    times, _, rows = outs[0].shape
    for n, out in enumerate(outs):
        for t in range(times):
            at = (n * times + t) * rows
            out[t] = total[:, at : at + rows].astype(out.dtype)


def total(factor, times, count, own, others):
    width, both = own.shape
    dims = (times, width, both // (times * count))
    return call(
        "total",
        functools.partial(total_kernel, factor, count),
        [VMEM] * (1 + len(others)),
        [shape(dims, jnp.float32)] + [shape(dims, jnp.bfloat16)] * (count - 1),
        (own, *others),
    )


def choose_kernel(own_ref, got_ref, out_ref):
    place = lax.axis_index("aux")
    inner = (place == 1) | (place == 2)
    out_ref[...] = jnp.where(inner, own_ref[...], got_ref[...].astype(jnp.float32))


def choose(own, got):
    return call("choose", choose_kernel, [VMEM] * 2, shape(own.shape, own.dtype), (own, got))


def shifted(x, axis, by):
    devices = lax.axis_size(axis)
    pairs = [(i, i + by) for i in range(devices) if 0 <= i + by < devices]
    return lax.ppermute(x, axis, pairs)


def body(three_center, occ_green, virt_band, tile_mask):
    rows, window, cols = three_center.shape
    times = virt_band.shape[0]
    tile = virt_band.shape[2] // 3
    planes, blocks = lax.axis_size("aux"), lax.axis_size("ao")
    chips = blocks // 2
    width = planes * rows // blocks
    factor = 1.0 / math.sqrt(window * cols * blocks)
    mates = [(i, i ^ 1) for i in range(blocks)]
    nexts = [(i, (i + 1 if i % 2 else i - 1) % blocks) for i in range(blocks)]

    def halo(full):
        inner, outer = edge(True, full, tile), edge(False, full, tile)
        return lax.ppermute(inner, "ao", mates), lax.ppermute(outer, "ao", nexts)

    occ = occ_green.transpose(1, 0, 2)
    mask = tile_mask.astype(jnp.bfloat16)[None, :, None, :, None]
    split = (window, rows // tile, tile, cols // tile, tile)
    own = three_center.transpose(1, 0, 2).reshape(split) * mask
    own = own.reshape(window, rows, cols)
    if planes == 4:
        swap = [(0, 1), (1, 0), (2, 3), (3, 2)]
        across = lax.ppermute(own, "aux", [(1, 2), (2, 1), (0, 0), (3, 3)])
        beside = lax.ppermute(own, "aux", swap)
        second = lax.ppermute(own, "aux", [(0, 2), (3, 1), (1, 0), (2, 3)])
        facing = edge(False, beside, tile)
        dressed = [dress(occ, own, *halo(own), virt_band, tile, (facing,))]
        outer = lax.ppermute(facing, "ao", nexts)
        inner = lax.ppermute(edge(True, beside, tile, dressed), "ao", mates)
        dressed.append(dress(occ, beside, inner, outer, virt_band, tile))
        near = {0: (lambda z: z, own), 1: (lambda z: z ^ 1, beside)}
        far = {3: (lambda z: z ^ 2, second), 2: (lambda z: 3 - z, across)}
    else:
        held = {0: own}
        for d in range(1, planes):
            hop, part = (d + 1) // 2, d // 2
            held[d] = shifted(held[part], "aux", -hop)
            held[-d] = shifted(held[-part], "aux", hop)
        dressed = [dress(occ, own, *halo(own), virt_band, tile)]
        plan = {d: (lambda z, d=d: z + d, block) for d, block in held.items()}
        near = {d: plan[d] for d in plan if abs(d) < 2}
        far = {d: plan[d] for d in plan if abs(d) >= 2}
    sums = ()
    for group in (near, far):
        if group:
            sources, held = zip(*group.values())
            sums = share(sources, chips, width, dressed, held, sums)
    keep, send = sums
    mine, *others = pair(keep, lax.ppermute(send, "ao", mates))
    others = [
        lax.ppermute(other, "ao", [(i, i ^ (2 * k)) for i in range(blocks)])
        for k, other in zip(farthest_first(chips), others)
    ]
    outs = total(factor, times, len(dressed), mine, others)
    if planes == 4:
        out = choose(outs[0], lax.ppermute(outs[1], "aux", swap))
    else:
        out = outs[0]
    return out.transpose(0, 2, 1)


def solution(mesh):
    in_specs = (P("aux", None, "ao"), P(), P(None, "ao", None), P("aux", "ao"))
    out_specs = P(None, "aux", "ao")
    return jax.shard_map(body, mesh=mesh, in_specs=in_specs, out_specs=out_specs, check_vma=False)
```

```python
import functools
import math

import jax
import jax.numpy as jnp
from jax import lax
from jax.experimental import pallas as pl
from jax.experimental.pallas import tpu as pltpu
from jax.sharding import PartitionSpec as P

VMEM = pl.BlockSpec(memory_space=pltpu.VMEM)
PARAMS = pltpu.CompilerParams(vmem_limit_bytes=16 * 1024 * 1024)
NT = (((1,), (1,)), ((), ()))


def shape(dims, dtype):
    return jax.ShapeDtypeStruct(dims, dtype)


def call(name, body, specs, outs, args):
    single = not isinstance(outs, (list, tuple))
    return pl.pallas_call(
        body,
        out_shape=outs,
        in_specs=specs,
        out_specs=VMEM if single else [VMEM] * len(outs),
        compiler_params=PARAMS,
        name=name,
    )(*args)


def is_even():
    return lax.rem(lax.axis_index("ao"), 2) == 0


def edge_kernel(tile, inner, full_ref, *refs):
    out_ref = refs[-1]
    window, _, cols = full_ref.shape
    at_end = is_even() if inner else jnp.logical_not(is_even())
    for l in range(window):
        first, last = full_ref[l, :, :tile], full_ref[l, :, cols - tile :]
        out_ref[l] = jnp.where(at_end, last, first)


def edge(inner, full, tile, after=()):
    window, rows, cols = full.shape
    return pl.pallas_call(
        functools.partial(edge_kernel, tile, inner),
        out_shape=shape((window, rows, tile), full.dtype),
        in_specs=[VMEM] + [pl.BlockSpec(memory_space=pl.ANY)] * len(after),
        out_specs=VMEM,
        compiler_params=PARAMS,
        name="edge",
    )(full, *after)


def dress_kernel(tile, occ_ref, own_ref, inner_ref, outer_ref, band_ref, *refs):
    out_ref = refs[-1]
    window, rows, cols = own_ref.shape
    times = band_ref.shape[0]
    count = cols // tile
    place = lax.axis_index("ao")
    even = is_even()
    inside = ((place != 0) & (place != lax.axis_size("ao") - 1)).astype(jnp.float32)
    tiles = [[] for _ in range(count + 2)]
    for m in range(window):
        inner = inner_ref[m].astype(jnp.float32)
        outer = outer_ref[m].astype(jnp.float32) * inside
        tiles[0].append(jnp.where(even, outer, inner))
        tiles[-1].append(jnp.where(even, inner, outer))
        for i in range(count):
            tiles[i + 1].append(own_ref[m, :, pl.ds(i * tile, tile)].astype(jnp.float32))
    green = [occ_ref[l].astype(jnp.float32) for l in range(window)]
    for t in range(times):
        products = []
        for l in range(window):
            row = []
            gains = [
                jnp.broadcast_to(green[l][t : t + 1, m : m + 1], (rows, tile))
                for m in range(window)
            ]
            for group in tiles:
                total = gains[0] * group[0]
                for m in range(1, window):
                    total = total + gains[m] * group[m]
                row.append(total.astype(jnp.bfloat16))
            products.append(jnp.concatenate(row, axis=1))
        tall = jnp.concatenate(products, axis=0)
        for i in range(count):
            value = lax.dot_general(
                tall[:, i * tile : (i + 3) * tile],
                band_ref[t, pl.ds(i * tile, tile), :],
                NT,
                preferred_element_type=jnp.float32,
            ).astype(jnp.bfloat16)
            for l in range(window):
                out_ref[pl.ds(t * rows, rows), pl.ds(l * cols + i * tile, tile)] = value[
                    l * rows : (l + 1) * rows
                ]


def dress(occ, own, inner, outer, band, tile, after=()):
    window, rows, cols = own.shape
    times = band.shape[0]
    return call(
        "dress",
        functools.partial(dress_kernel, tile),
        [VMEM] * 5 + [pl.BlockSpec(memory_space=pl.ANY)] * len(after),
        shape((times * rows, window * cols), jnp.bfloat16),
        (occ, own, inner, outer, band, *after),
    )


def share_kernel(sources, width, parts, *refs):
    count = len(sources)
    dressed, blocks = refs[:parts], refs[parts : parts + count]
    earlier = refs[parts + count : -2]
    keep_ref, send_ref = refs[-2:]
    window, rows, _ = blocks[0].shape
    planes = lax.axis_size("aux")
    place = lax.axis_index("aux")
    even = is_even()
    if earlier:
        keep_ref[...] = earlier[0][...]
        send_ref[...] = earlier[1][...]
    per = rows // (2 * width)

    def flat(block):
        return jnp.concatenate([block[l] for l in range(window)], axis=1)

    def put(total, source, here):
        for j in range(per):
            low = total[2 * j * width : (2 * j + 1) * width]
            high = total[(2 * j + 1) * width : (2 * j + 2) * width]
            row = source * per + j
            keep_ref[row, :, here] = jnp.where(even, low, high)
            send_ref[row, :, here] = jnp.where(even, high, low).astype(jnp.bfloat16)

    at = 0
    for left in dressed:
        here = pl.ds(at, left.shape[0])
        at += left.shape[0]
        if parts > 1:
            tall = jnp.concatenate([flat(block) for block in blocks], axis=0)
            total = lax.dot_general(tall, left[...], NT, preferred_element_type=jnp.float32)
            for n, source_of in enumerate(sources):
                put(total[n * rows : (n + 1) * rows], source_of(place), here)
            continue
        for source_of, block in zip(sources, blocks):
            source = source_of(place)

            @pl.when((source >= 0) & (source < planes))
            def _(block=block, source=source, left=left, here=here):
                put(
                    lax.dot_general(
                        flat(block), left[...], NT, preferred_element_type=jnp.float32
                    ),
                    source,
                    here,
                )


def share(sources, chips, width, dressed, blocks, earlier):
    dims = (chips, width, sum(d.shape[0] for d in dressed))
    args = [*dressed, *blocks, *earlier]
    return call(
        "share",
        functools.partial(share_kernel, sources, width, len(dressed)),
        [VMEM] * len(args),
        [shape(dims, jnp.float32), shape(dims, jnp.bfloat16)],
        args,
    )


def farthest_first(chips):
    return range(chips - 1, 0, -1)


def pair_kernel(parts, keep_ref, got_ref, *outs):
    chips, _, both = keep_ref.shape
    chip = lax.axis_index("ao") // 2
    size = both // parts
    for n in range(parts):
        here = pl.ds(n * size, size)
        for k, out in zip((0, *farthest_first(chips)), outs[n * chips : (n + 1) * chips]):
            other = chip ^ k
            value = keep_ref[other, :, here] + got_ref[other, :, here].astype(jnp.float32)
            out[...] = value.astype(out.dtype)


def pair(parts, keep, got):
    chips, width, both = keep.shape
    dims = (width, both // parts)
    kinds = ([jnp.float32] + [jnp.bfloat16] * (chips - 1)) * parts
    outs = call(
        "pair",
        functools.partial(pair_kernel, parts),
        [VMEM] * 2,
        [shape(dims, kind) for kind in kinds],
        (keep, got),
    )
    return [outs[n * chips : (n + 1) * chips] for n in range(parts)]


def total_kernel(factor, count, *refs):
    terms, back, out_ref = refs[:count], refs[count:-1], refs[-1]
    value = terms[0][...]
    for term in terms[1:]:
        value += term[...].astype(jnp.float32)
    value *= factor
    place = lax.axis_index("aux")
    inner = (place > 0) & (place < lax.axis_size("aux") - 1)
    times, _, rows = out_ref.shape
    for t in range(times):
        part = value[:, t * rows : (t + 1) * rows]
        for ref in back:
            part = jnp.where(inner, part, ref[t].astype(jnp.float32))
        out_ref[t] = part.astype(out_ref.dtype)


def total(factor, times, kind, terms, back=()):
    width, both = terms[0].shape
    return call(
        "total",
        functools.partial(total_kernel, factor, len(terms)),
        [VMEM] * (len(terms) + len(back)),
        shape((times, width, both // times), kind),
        (*terms, *back),
    )


def shifted(x, axis, by):
    devices = lax.axis_size(axis)
    pairs = [(i, i + by) for i in range(devices) if 0 <= i + by < devices]
    return lax.ppermute(x, axis, pairs)


def body(three_center, occ_green, virt_band, tile_mask):
    rows, window, cols = three_center.shape
    times = virt_band.shape[0]
    tile = virt_band.shape[2] // 3
    planes, blocks = lax.axis_size("aux"), lax.axis_size("ao")
    chips = blocks // 2
    width = planes * rows // blocks
    factor = 1.0 / math.sqrt(window * cols * blocks)
    mates = [(i, i ^ 1) for i in range(blocks)]
    nexts = [(i, (i + 1 if i % 2 else i - 1) % blocks) for i in range(blocks)]

    def halo(full):
        inner, outer = edge(True, full, tile), edge(False, full, tile)
        return lax.ppermute(inner, "ao", mates), lax.ppermute(outer, "ao", nexts)

    occ = occ_green.transpose(1, 0, 2)
    mask = tile_mask.astype(jnp.bfloat16)[None, :, None, :, None]
    split = (window, rows // tile, tile, cols // tile, tile)
    own = three_center.transpose(1, 0, 2).reshape(split) * mask
    own = own.reshape(window, rows, cols)
    if planes == 4:
        swap = [(0, 1), (1, 0), (2, 3), (3, 2)]
        across = lax.ppermute(own, "aux", [(1, 2), (2, 1), (0, 0), (3, 3)])
        beside = lax.ppermute(own, "aux", swap)
        second = lax.ppermute(own, "aux", [(0, 2), (3, 1), (1, 0), (2, 3)])
        facing = edge(False, beside, tile)
        dressed = [dress(occ, own, *halo(own), virt_band, tile, (facing,))]
        outer = lax.ppermute(facing, "ao", nexts)
        inner = lax.ppermute(edge(True, beside, tile, dressed), "ao", mates)
        dressed.append(dress(occ, beside, inner, outer, virt_band, tile))
        near = {0: (lambda z: z, own), 1: (lambda z: z ^ 1, beside)}
        far = {3: (lambda z: z ^ 2, second), 2: (lambda z: 3 - z, across)}
    else:
        held = {0: own}
        for d in range(1, planes):
            hop, part = (d + 1) // 2, d // 2
            held[d] = shifted(held[part], "aux", -hop)
            held[-d] = shifted(held[-part], "aux", hop)
        dressed = [dress(occ, own, *halo(own), virt_band, tile)]
        plan = {d: (lambda z, d=d: z + d, block) for d, block in held.items()}
        near = {d: plan[d] for d in plan if abs(d) < 2}
        far = {d: plan[d] for d in plan if abs(d) >= 2}
    sums = ()
    for group in (near, far):
        if group:
            sources, held = zip(*group.values())
            sums = share(sources, chips, width, dressed, held, sums)
    keep, send = sums
    def exchanged(terms):
        others = [
            lax.ppermute(other, "ao", [(i, i ^ (2 * k)) for i in range(blocks)])
            for k, other in zip(farthest_first(chips), terms[1:])
        ]
        return [terms[0], *others]

    groups = pair(len(dressed), keep, lax.ppermute(send, "ao", mates))
    back = [
        lax.ppermute(total(factor, times, jnp.bfloat16, exchanged(terms)), "aux", swap)
        for terms in groups[1:]
    ]
    out = total(factor, times, jnp.float32, exchanged(groups[0]), back)
    return out.transpose(0, 2, 1)


def solution(mesh):
    in_specs = (P("aux", None, "ao"), P(), P(None, "ao", None), P("aux", "ao"))
    out_specs = P(None, "aux", "ao")
    return jax.shard_map(body, mesh=mesh, in_specs=in_specs, out_specs=out_specs, check_vma=False)
```
